768 devices in a mesh: occ: 96 (over x, y, z_hi), aux: 8 (over z_lo, core).
Axes of the slice: x: 4, y: 8, z: 12 (z_hi: 3, z_lo: 4; z = z_hi * 4 + z_lo), core: 2. Of those that a mesh axis runs over, the one named last changes fastest.
Arguments:
- factors: float32 [96, 3072, 512], P('occ', 'aux'), may hold values from -0.8 to 0.8
- occ_energy: float32 [96], P('occ'), may hold values from -1.5 to -0.5
- virt_energy: float32 [512], replicated, may hold values from 0.2 to 3
Outputs:
- density: float32 [96, 3072, 512], P('occ', 'aux')
The draws below stay inside these ranges and needn't reach their ends.
All inputs are finite; a program needn't handle non-finite values.
Results may differ from the reference program's by a relative error of at most 0.000052.
Values sent between devices are 32-bit elements; how exact they have to be, the bound alone decides.
No kernel may reach another device: no remote copies, remote signals or barrier semaphores. Data moves between devices by JAX's collectives and lax.ppermute only.
A program may use at most 32 MiB of HBM per device.

```python
import jax
import jax.numpy as jnp
from jax import lax

VIRT = 512
NAUX = 3072
NOCC = 96


def levels(stream_key, shape, cuts, least, top_value):
    def one(position, shards_of):
        heights = jax.random.uniform(jax.random.fold_in(jax.random.fold_in(stream_key, 6), position), (shards_of,), jnp.float32, least / len(cuts), top_value / len(cuts))
        return jnp.repeat(jnp.exp(heights), shape[position] // shards_of).reshape((-1,) + (1,) * (len(shape) - position - 1))

    level = one(*cuts[0])
    for cut in cuts[1:]:
        level = level * one(*cut)
    return level


def centred(own_key, dims, width, reach, cuts=(), dtype=jnp.bfloat16):
    entries = width * jax.random.normal(own_key, dims, jnp.float32)
    if cuts:
        entries = entries * levels(own_key, dims, cuts, -0.22, 0.18)
    return jnp.clip(entries, -reach, reach).astype(dtype)


def setup_inputs(seed: int = 0) -> dict:
    keys = jax.random.split(jax.random.key(seed), 4)
    factors = centred(keys[0], (NOCC, NAUX, VIRT), 0.13, 0.8, ((0, 96), (1, 8)), jnp.float32)
    occ_energy = jnp.clip(-1.5 + 1.0 * jax.random.uniform(keys[1], (NOCC,), jnp.float32) ** levels(keys[1], (NOCC,), ((0, 96),), -0.2, 0.2), -1.5, -0.5)
    virt_energy = jnp.clip(jax.random.uniform(keys[2], (VIRT,), jnp.float32, 0.2, 3.0), 0.2, 3.0)
    return {"factors": factors, "occ_energy": occ_energy, "virt_energy": virt_energy}


def reference(factors, occ_energy, virt_energy):
    prev_f = jnp.roll(factors, 1, axis=0)
    next_f = jnp.roll(factors, -1, axis=0)
    prev_e = jnp.roll(occ_energy, 1, axis=0)
    pair = jnp.einsum("iqa,iqb->iab", factors, prev_f, precision=lax.Precision.HIGHEST, preferred_element_type=jnp.float32)
    denom = virt_energy[None, :, None] + virt_energy[None, None, :] - (occ_energy + prev_e)[:, None, None]
    amplitude = pair / denom
    next_amp = jnp.roll(amplitude, -1, axis=0)
    own = jnp.einsum("iqb,iab->iqa", prev_f, amplitude, precision=lax.Precision.HIGHEST, preferred_element_type=jnp.float32)
    other = jnp.einsum("iqc,ica->iqa", next_f, next_amp, precision=lax.Precision.HIGHEST, preferred_element_type=jnp.float32)
    return own + other
```

```python
import jax
import jax.numpy as jnp
from jax import lax
from jax.sharding import Mesh, PartitionSpec as P

CHIPS = 4


def cells(fn, occupied):
    pairs = []
    for i in range(occupied):
        for z in range(CHIPS):
            for h in range(2):
                j, w, k = fn(i, z, h)
                pairs.append(((i * CHIPS + z) * 2 + h, ((j % occupied) * CHIPS + w) * 2 + k))
    return pairs


ALL = ("occ", "z", "core")


def along_occ(x, by, cross):
    n = lax.axis_size("occ")
    return lax.ppermute(x, ALL, cells(lambda i, z, h: (i + by, z, h ^ cross), n))


def core_swap(x):
    return lax.ppermute(x, "core", [(0, 1), (1, 0)])


def local(factors, occ_energy, virt_energy):
    own = factors[0]
    rows, virt = own.shape
    half, quarter = virt // 2, virt // CHIPS
    core = lax.axis_index("core")
    z = lax.axis_index("z")

    same = lax.dynamic_slice_in_dim(own, core * half, half, 1)
    cross = lax.dynamic_slice_in_dim(own, (1 - core) * half, half, 1)
    low_same = along_occ(same, 1, 0)
    up_same = along_occ(same, -1, 0)
    low_cross = along_occ(cross, 1, 1)
    up_cross = along_occ(cross, -1, 1)
    other = core_swap(own)
    energy, other = lax.optimization_barrier((occ_energy, other))
    lower_energy = along_occ(energy, 1, 0)
    upper_energy = along_occ(energy, -1, 0)

    left = jnp.concatenate([own, other])
    right = jnp.concatenate(
        [jnp.concatenate([low_same, up_same], 1), jnp.concatenate([low_cross, up_cross], 1)]
    )
    tile = jnp.einsum("qa,qn->an", left, right, precision=lax.Precision.HIGH, preferred_element_type=jnp.float32)
    parts = lax.all_to_all(tile.reshape(CHIPS, quarter, virt), "z", 0, 0, tiled=True)
    total = (parts[0] + parts[1]) + (parts[2] + parts[3])
    row_energy = lax.dynamic_slice_in_dim(virt_energy, z * quarter, quarter, 0)
    half_energy = lax.dynamic_slice_in_dim(virt_energy, core * half, half, 0)
    column_energy = jnp.concatenate(
        [half_energy - (occ_energy + lower_energy), half_energy - (upper_energy + occ_energy)]
    )
    amps = total / (row_energy[:, None] + column_energy[None, :])
    pieces = [amps] + [lax.ppermute(amps, "z", [(k, k ^ d) for k in range(CHIPS)]) for d in (1, 2, 3)]
    def place(d):
        return lax.dynamic_index_in_dim(stacked, z ^ d, 0, keepdims=False)

    stacked = jnp.stack(pieces)
    whole = jnp.concatenate([place(d) for d in range(CHIPS)])
    partial = jnp.einsum("qn,an->qa", right, whole, precision=lax.Precision.HIGH, preferred_element_type=jnp.float32)
    return (partial[:rows] + core_swap(partial[rows:]))[None]


def solution(mesh):
    cube = Mesh(mesh.devices.reshape(mesh.devices.shape[0], CHIPS, 2), ALL)
    spec = P("occ", ("z", "core"), None)
    return jax.shard_map(local, mesh=cube, in_specs=(spec, P("occ"), P()), out_specs=spec, check_vma=False)
```

```python
import jax
import jax.numpy as jnp
from jax import lax
from jax.sharding import Mesh, PartitionSpec as P

CHIPS = 4
ALL = ("occ", "z", "core")
PRECISION = lax.Precision.HIGH


def along_occ(x, by):
    n = lax.axis_size("occ")
    return lax.ppermute(x, "occ", [(i, (i + by) % n) for i in range(n)])


def core_swap(x):
    return lax.ppermute(x, "core", [(0, 1), (1, 0)])


def local(factors, occ_energy, virt_energy):
    own = factors[0]
    rows, virt = own.shape
    half, quarter = virt // 2, virt // CHIPS
    core = lax.axis_index("core")
    z = lax.axis_index("z")

    chip = jnp.concatenate([own, core_swap(own)])
    columns = lax.dynamic_slice_in_dim(chip, core * half, half, 1)
    parcel = jnp.concatenate([columns, jnp.broadcast_to(occ_energy, (8, half))])
    lower = along_occ(parcel, 1)
    upper = along_occ(parcel, -1)
    right = jnp.concatenate([lower[: 2 * rows], upper[: 2 * rows]], 1)
    tile = jnp.einsum("qa,qn->an", chip, right, precision=PRECISION, preferred_element_type=jnp.float32)
    parts = lax.all_to_all(tile.reshape(CHIPS, quarter, virt), "z", 0, 0, tiled=True)
    total = (parts[0] + parts[1]) + (parts[2] + parts[3])
    row_energy = lax.dynamic_slice_in_dim(virt_energy, z * quarter, quarter, 0)
    half_energy = lax.dynamic_slice_in_dim(virt_energy, core * half, half, 0)
    column_energy = jnp.concatenate(
        [half_energy - (occ_energy + lower[2 * rows, 0]), half_energy - (upper[2 * rows, 0] + occ_energy)]
    )
    amps = total / (row_energy[:, None] + column_energy[None, :])
    whole = lax.all_to_all(jnp.broadcast_to(amps, (CHIPS, quarter, virt)), "z", 0, 0, tiled=True)
    whole = whole.reshape(virt, virt)
    partial = jnp.einsum("qn,an->qa", right, whole, precision=PRECISION, preferred_element_type=jnp.float32)
    return (partial[:rows] + core_swap(partial[rows:]))[None]


def solution(mesh):
    cube = Mesh(mesh.devices.reshape(mesh.devices.shape[0], CHIPS, 2), ALL)
    spec = P("occ", ("z", "core"), None)
    return jax.shard_map(local, mesh=cube, in_specs=(spec, P("occ"), P()), out_specs=spec, check_vma=False)
```

```python
import jax
import jax.numpy as jnp
from jax import lax
from jax.experimental import pallas as pl
from jax.experimental.pallas import tpu as pltpu
from jax.sharding import Mesh, PartitionSpec as P

CHIPS = 4
ALL = ("occ", "z", "core")
SMEM = pl.BlockSpec(memory_space=pltpu.SMEM)
VMEM = pl.BlockSpec(memory_space=pltpu.VMEM)
ANY = pl.BlockSpec(memory_space=pl.ANY)


def along_occ(x, by, cross=0):
    n = lax.axis_size("occ")
    pairs = [
        ((i * CHIPS + z) * 2 + h, ((i + by) % n * CHIPS + z) * 2 + (h ^ cross))
        for i in range(n)
        for z in range(CHIPS)
        for h in range(2)
    ]
    return lax.ppermute(x, ALL, pairs)


def core_swap(x):
    return lax.ppermute(x, "core", [(0, 1), (1, 0)])


def kernel(body, shapes, scalars, arrays, after=(), flops=0):
    used = len(scalars) + len(arrays)

    def run(*refs):
        body(*refs[:used], *refs[used + len(after) :])

    return pl.pallas_call(
        run,
        out_shape=[jax.ShapeDtypeStruct(s, jnp.float32) for s in shapes],
        in_specs=[SMEM] * len(scalars) + [VMEM] * len(arrays) + [ANY] * len(after),
        out_specs=[VMEM] * len(shapes),
        cost_estimate=pl.CostEstimate(flops=flops, bytes_accessed=0, transcendentals=0),
        compiler_params=pltpu.CompilerParams(vmem_limit_bytes=40 * 2**20),
    )(*[s.reshape(1) for s in scalars], *arrays, *after)


def split(x):
    high = x.astype(jnp.bfloat16)
    return high, (x - high.astype(jnp.float32)).astype(jnp.bfloat16)


def dot(x, y, dims):
    x_high, x_low = split(x)
    y_high, y_low = split(y)

    def one(u, v):
        return lax.dot_general(u, v, (dims, ((), ())), preferred_element_type=jnp.float32)

    return one(x_high, y_high) + (one(x_high, y_low) + one(x_low, y_high))


def pair_tile(own_ref, other_ref, near_ref, far_ref, out_ref):
    rows = own_ref.shape[0]
    chip = jnp.concatenate([own_ref[...], other_ref[...]])
    right = jnp.concatenate([near_ref[:rows], far_ref[...]])
    out_ref[...] = dot(chip, right, ((0,), (0,))).reshape(out_ref.shape)


def divide(parts_ref, denominator_ref, tile_ref, out_ref):
    total = (parts_ref[0] + parts_ref[1]) + (parts_ref[2] + parts_ref[3])
    amplitude = total / denominator_ref[...]
    tile_ref[...] = amplitude
    for k in range(CHIPS):
        out_ref[k] = amplitude


def repeat(tile_ref, out_ref):
    for k in range(CHIPS):
        out_ref[k] = tile_ref[...]


def lower_part(near_ref, far_ref, amp_ref, mine_ref, others_ref):
    rows, virt = mine_ref.shape
    right = jnp.concatenate([near_ref[:rows], far_ref[...]])
    product = dot(right, amp_ref[...].reshape(virt, -1), ((1,), (1,)))
    mine_ref[...] = product[:rows]
    others_ref[...] = product[rows:]


def upper_part(here_ref, up_ref, up_other_ref, amp_ref, mine_ref, others_ref, out_ref, out_others_ref):
    rows, virt = mine_ref.shape
    chip = jnp.concatenate([up_ref[...], up_other_ref[...]])
    product = dot(chip, amp_ref[...].reshape(virt, -1), ((1,), (0,)))
    width = product.shape[1]
    columns = pl.ds(pl.multiple_of(here_ref[0], width), width)
    out_ref[...] = mine_ref[...]
    out_ref[:, columns] += product[:rows]
    out_others_ref[...] = others_ref[...]
    out_others_ref[:, columns] += product[rows:]


def local(factors, occ_energy, virt_energy):
    own = factors[0]
    rows, virt = own.shape
    half, quarter = virt // 2, virt // CHIPS
    core = lax.axis_index("core")
    z = lax.axis_index("z")
    here = core * half

    def columns(start):
        return lax.dynamic_slice_in_dim(own, start, half, 1)

    def shared(x):
        return lax.all_to_all(x, "z", 0, 0, tiled=True)

    near = along_occ(jnp.concatenate([columns(here), jnp.broadcast_to(occ_energy, (8, half))]), 1)
    far = along_occ(columns(half - here), 1, cross=1)
    upper = along_occ(own, -1)
    other = core_swap(own)
    upper_other = core_swap(upper)

    row_energy = lax.dynamic_slice_in_dim(virt_energy, z * quarter, quarter, 0) - (occ_energy + near[rows, 0])
    denominator = row_energy[:, None] + lax.dynamic_slice_in_dim(virt_energy, here, half, 0)[None, :]

    whole = (CHIPS, quarter, half)
    parts = shared(kernel(pair_tile, [whole], [], [own, other, near, far])[0])
    tile, copies = kernel(divide, [(quarter, half), whole], [], [parts, denominator], (upper_other,))
    upper_tile = along_occ(tile, -1)
    amp = shared(copies)
    upper_amp = shared(kernel(repeat, [whole], [], [upper_tile])[0])
    slab = (rows, virt)
    mine, others = kernel(lower_part, [slab] * 2, [], [near, far, amp])
    mine, others = kernel(upper_part, [slab] * 2, [here], [upper, upper_other, upper_amp, mine, others])
    return (mine + core_swap(others))[None]


def solution(mesh):
    cube = Mesh(mesh.devices.reshape(mesh.devices.shape[0], CHIPS, 2), ALL)
    spec = P("occ", ("z", "core"), None)
    return jax.shard_map(local, mesh=cube, in_specs=(spec, P("occ"), P()), out_specs=spec, check_vma=False)
```

```python
import jax
import jax.numpy as jnp
from jax import lax
from jax.experimental import pallas as pl
from jax.experimental.pallas import tpu as pltpu
from jax.sharding import Mesh, PartitionSpec as P

CHIPS = 4
ALL = ("occ", "z", "core")
SMEM = pl.BlockSpec(memory_space=pltpu.SMEM)
VMEM = pl.BlockSpec(memory_space=pltpu.VMEM)
ANY = pl.BlockSpec(memory_space=pl.ANY)


def along_occ(x, by, cross=0):
    n = lax.axis_size("occ")
    pairs = [
        ((i * CHIPS + z) * 2 + h, ((i + by) % n * CHIPS + z) * 2 + (h ^ cross))
        for i in range(n)
        for z in range(CHIPS)
        for h in range(2)
    ]
    return lax.ppermute(x, ALL, pairs)


def core_swap(x):
    return lax.ppermute(x, "core", [(0, 1), (1, 0)])


def kernel(body, shapes, scalars, arrays, after=(), flops=0):
    used = len(scalars) + len(arrays)

    def run(*refs):
        body(*refs[:used], *refs[used + len(after) :])

    return pl.pallas_call(
        run,
        out_shape=[jax.ShapeDtypeStruct(s, jnp.float32) for s in shapes],
        in_specs=[SMEM] * len(scalars) + [VMEM] * len(arrays) + [ANY] * len(after),
        out_specs=[VMEM] * len(shapes),
        cost_estimate=pl.CostEstimate(flops=flops, bytes_accessed=0, transcendentals=0),
        compiler_params=pltpu.CompilerParams(vmem_limit_bytes=24 * 2**20),
    )(*[s.reshape(1) for s in scalars], *arrays, *after)


def split(x):
    high = x.astype(jnp.bfloat16)
    return high, (x - high.astype(jnp.float32)).astype(jnp.bfloat16)


def dot(x, y, dims):
    def one(u, v):
        return lax.dot_general(u, v, (dims, ((), ())), preferred_element_type=jnp.float32)

    return one(x[0], y[0]) + (one(x[0], y[1]) + one(x[1], y[0]))


ROWS = ((0,), (0,))
LAST = ((1,), (1,))
PLAIN = ((1,), (0,))


def block(start_ref, width):
    return pl.ds(pl.multiple_of(start_ref[0], width), width)


def pair_tiles(here_ref, there_ref, own_ref, other_ref, low_ref, low_far_ref, up_ref, up_far_ref, out_ref):
    rows, width = low_far_ref.shape
    here, there = block(here_ref, width), block(there_ref, width)
    chip_here = split(jnp.concatenate([own_ref[:, here], other_ref[:, here]]))
    chip_there = split(jnp.concatenate([own_ref[:, there], other_ref[:, there]]))
    lower = split(jnp.concatenate([low_ref[:rows], low_far_ref[...]]))
    upper = split(jnp.concatenate([up_ref[:rows], up_far_ref[...]]))
    part = (CHIPS, width // CHIPS, width)
    out_ref[:, :, :width] = dot(chip_there, lower, ROWS).reshape(part)
    out_ref[:, :, width:] = dot(upper, chip_here, ROWS).reshape(part)


def divide(parts_ref, denominator_ref, low_ref, up_ref):
    total = (parts_ref[0] + parts_ref[1]) + (parts_ref[2] + parts_ref[3])
    amplitude = total / denominator_ref[...]
    width = low_ref.shape[1]
    low_ref[...] = amplitude[:, :width]
    up_ref[...] = amplitude[:, width:]


def lay_out(*refs):
    out_ref = refs[-1]
    width = refs[0].shape[1]
    for n, ref in enumerate(refs[:-1]):
        for k in range(CHIPS):
            out_ref[k, :, n * width : (n + 1) * width] = ref[...]


def density_part(here_ref, there_ref, low_ref, low_far_ref, up_ref, up_far_ref, amps_ref, mine_ref, others_ref):
    rows, width = low_far_ref.shape
    lower = split(jnp.concatenate([low_ref[:rows], low_far_ref[...]]))
    upper = split(jnp.concatenate([up_ref[:rows], up_far_ref[...]]))
    amps = amps_ref[...].reshape(width, 4 * width)
    low_there, up_here, low_here, up_there = (split(amps[:, n * width : (n + 1) * width]) for n in range(4))
    for start_ref, low_amp, up_amp in ((here_ref, low_here, up_here), (there_ref, low_there, up_there)):
        product = dot(lower, low_amp, LAST) + dot(upper, up_amp, PLAIN)
        columns = block(start_ref, width)
        mine_ref[:, columns] = product[:rows]
        others_ref[:, columns] = product[rows:]


def local(factors, occ_energy, virt_energy):
    own = factors[0]
    rows, virt = own.shape
    half = virt // 2
    part = half // CHIPS
    core = lax.axis_index("core")
    z = lax.axis_index("z")
    here = core * half
    there = half - here

    def columns(start):
        return lax.dynamic_slice_in_dim(own, start, half, 1)

    def energies(start, length):
        return lax.dynamic_slice_in_dim(virt_energy, start, length, 0)

    def shared(x):
        return lax.all_to_all(x, "z", 0, 0, tiled=True)

    near = jnp.concatenate([columns(here), jnp.broadcast_to(occ_energy, (8, half))])
    far = columns(there)
    low, up = along_occ(near, 1), along_occ(near, -1)
    low_far, up_far = along_occ(far, 1, cross=1), along_occ(far, -1, cross=1)
    other = core_swap(own)

    def denominator(rows_start, neighbour):
        row_energy = energies(rows_start + z * part, part) - (occ_energy + neighbour[rows, 0])
        return row_energy[:, None] + energies(here, half)[None, :]

    tiles = kernel(
        pair_tiles, [(CHIPS, part, virt)], [here, there], [own, other, low, low_far, up, up_far]
    )[0]
    denominators = jnp.concatenate([denominator(there, low), denominator(here, up)], 1)
    low_tile, up_tile = kernel(divide, [(part, half)] * 2, [], [shared(tiles), denominators])
    low_rest, up_rest = along_occ(up_tile, 1), along_occ(low_tile, -1, cross=1)
    whole = kernel(lay_out, [(CHIPS, part, 2 * virt)], [], [low_tile, up_tile, low_rest, up_rest])[0]
    mine, others = kernel(
        density_part, [(rows, virt)] * 2, [here, there], [low, low_far, up, up_far, shared(whole)]
    )
    return (mine + core_swap(others))[None]


def solution(mesh):
    cube = Mesh(mesh.devices.reshape(mesh.devices.shape[0], CHIPS, 2), ALL)
    spec = P("occ", ("z", "core"), None)
    return jax.shard_map(local, mesh=cube, in_specs=(spec, P("occ"), P()), out_specs=spec, check_vma=False)
```

```python
import jax
import jax.numpy as jnp
from jax import lax
from jax.experimental import pallas as pl
from jax.experimental.pallas import tpu as pltpu
from jax.sharding import Mesh, PartitionSpec as P

CHIPS = 4
LEVELS = 3
RING = CHIPS * LEVELS
PLACES = ("occ", "z")
SMEM = pl.BlockSpec(memory_space=pltpu.SMEM)
VMEM = pl.BlockSpec(memory_space=pltpu.VMEM)


def meetings(occupied):
    columns = occupied // LEVELS
    above, below = [], []
    for place in range(occupied * CHIPS):
        column, height = divmod(place, RING)
        above.append(column * RING + (height + CHIPS // 2) % RING)
        shift = 1 if height < CHIPS else 0
        below.append((column - shift) % columns * RING + (height - CHIPS // 2) % RING)
    return above, below


def there(goals):
    return [(place, goal) for place, goal in enumerate(goals)]


def back(goals):
    return [(goal, place) for place, goal in enumerate(goals)]


def move(x, pairs):
    return lax.ppermute(x, PLACES, pairs)


def core_swap(x):
    return lax.ppermute(x, "core", [(0, 1), (1, 0)])


def kernel(body, shapes, scalars, arrays):
    return pl.pallas_call(
        body,
        out_shape=[jax.ShapeDtypeStruct(s, jnp.float32) for s in shapes],
        in_specs=[SMEM] * len(scalars) + [VMEM] * len(arrays),
        out_specs=[VMEM] * len(shapes),
        compiler_params=pltpu.CompilerParams(vmem_limit_bytes=24 * 2**20),
    )(*[s.reshape(1) for s in scalars], *arrays)


def split(x):
    high = x.astype(jnp.bfloat16)
    return high, (x - high.astype(jnp.float32)).astype(jnp.bfloat16)


def dot(x, y, dims):
    def one(u, v):
        return lax.dot_general(u, v, (dims, ((), ())), preferred_element_type=jnp.float32)

    return one(x[0], y[0]) + (one(x[0], y[1]) + one(x[1], y[0]))


def block(start_ref, width):
    return pl.ds(pl.multiple_of(start_ref[0], width), width)


def pair_tile(mine_ref, other_ref, lower_ref, upper_ref, keep_ref, give_ref):
    width = keep_ref.shape[1]
    rows = lower_ref.shape[0] - 8
    upper = split(upper_ref[:rows])
    for start_ref, out_ref in ((other_ref, give_ref), (mine_ref, keep_ref)):
        out_ref[...] = dot(upper, split(lower_ref[:rows, block(start_ref, width)]), ((0,), (0,)))


def add_tiles(keep_ref, got_ref, out_ref):
    out_ref[...] = (keep_ref[...] + got_ref[...]).reshape(out_ref.shape)


def divide(parts_ref, denominator_ref, out_ref):
    total = (parts_ref[0] + parts_ref[1]) + (parts_ref[2] + parts_ref[3])
    amplitude = total / denominator_ref[...]
    for k in range(CHIPS):
        out_ref[k] = amplitude


def density_parts(mine_ref, other_ref, lower_ref, upper_ref, amp_ref, swapped_ref, up_ref, down_ref):
    rows, virt = up_ref.shape
    width = amp_ref.shape[2]
    upper = split(upper_ref[:rows])
    total = None
    for start_ref, half_ref in ((mine_ref, amp_ref), (other_ref, swapped_ref)):
        columns = block(start_ref, width)
        amp = split(half_ref[...].reshape(virt, width))
        down_ref[:, columns] = dot(upper, amp, ((1,), (0,)))
        part = dot(split(lower_ref[:rows, columns]), amp, ((1,), (1,)))
        total = part if total is None else total + part
    up_ref[...] = total


def local(factors, occ_energy, virt_energy):
    own = factors[0]
    rows, virt = own.shape
    half, quarter = virt // 2, virt // CHIPS
    occupied = lax.axis_size("occ")
    above, below = meetings(occupied)
    groups = [
        [above[(level * CHIPS) + RING * column + c] for c in range(CHIPS)]
        for column in range(occupied // LEVELS)
        for level in range(LEVELS)
    ]
    mine = lax.axis_index("core") * half
    other = half - mine
    chip = lax.rem(lax.axis_index("z") + CHIPS // 2, CHIPS)

    def shared(x):
        return lax.all_to_all(x, PLACES, 0, 0, axis_index_groups=groups, tiled=True)

    parcel = jnp.concatenate([own, jnp.broadcast_to(occ_energy, (8, virt))])
    lower = move(parcel, there(above))
    upper = move(parcel, there(below))
    keep, give = kernel(pair_tile, [(virt, half)] * 2, [mine, other], [lower, upper])
    whole = (CHIPS, quarter, half)
    tile = kernel(add_tiles, [whole], [], [keep, core_swap(give)])[0]
    row_energy = lax.dynamic_slice_in_dim(virt_energy, chip * quarter, quarter, 0)
    column_energy = lax.dynamic_slice_in_dim(virt_energy, mine, half, 0)
    pair_energy = lower[rows, 0] + upper[rows, 0]
    denominator = (row_energy - pair_energy)[:, None] + column_energy[None, :]
    amp = shared(kernel(divide, [whole], [], [shared(tile), denominator])[0])
    up, down = kernel(density_parts, [(rows, virt)] * 2, [mine, other], [lower, upper, amp, core_swap(amp)])
    return (move(up, back(below)) + move(down, back(above)))[None]


def solution(mesh):
    cube = Mesh(mesh.devices.reshape(mesh.devices.shape[0], CHIPS, 2), (*PLACES, "core"))
    spec = P("occ", ("z", "core"), None)
    return jax.shard_map(local, mesh=cube, in_specs=(spec, P("occ"), P()), out_specs=spec, check_vma=False)
```

```python
import jax
import jax.numpy as jnp
from jax import lax
from jax.experimental import pallas as pl
from jax.experimental.pallas import tpu as pltpu
from jax.sharding import Mesh, PartitionSpec as P

CHIPS = 4
LEVELS = 3
RING = CHIPS * LEVELS
PLACES = ("occ", "z")
SMEM = pl.BlockSpec(memory_space=pltpu.SMEM)
VMEM = pl.BlockSpec(memory_space=pltpu.VMEM)
ANY = pl.BlockSpec(memory_space=pl.ANY)


def meetings(occupied):
    columns = occupied // LEVELS
    above, below = [], []
    for place in range(occupied * CHIPS):
        column, height = divmod(place, RING)
        above.append(column * RING + (height + CHIPS // 2) % RING)
        shift = 1 if height < CHIPS else 0
        below.append((column - shift) % columns * RING + (height - CHIPS // 2) % RING)
    return above, below


def in_two(above, below):
    up_first = [place % CHIPS < CHIPS // 2 for place in range(len(above))]
    first = [a if up else b for a, b, up in zip(above, below, up_first)]
    second = [b if up else a for a, b, up in zip(above, below, up_first)]
    return first, second


def there(goals):
    return [(place, goal) for place, goal in enumerate(goals)]


def back(goals):
    return [(goal, place) for place, goal in enumerate(goals)]


def move(x, pairs):
    return lax.ppermute(x, PLACES, pairs)


def core_swap(x):
    return lax.ppermute(x, "core", [(0, 1), (1, 0)])


def kernel(body, shapes, scalars, arrays, after=()):
    used = len(scalars) + len(arrays)

    def run(*refs):
        body(*refs[:used], *refs[used + len(after) :])

    return pl.pallas_call(
        run,
        out_shape=[jax.ShapeDtypeStruct(s, jnp.float32) for s in shapes],
        in_specs=[SMEM] * len(scalars) + [VMEM] * len(arrays) + [ANY] * len(after),
        out_specs=[VMEM] * len(shapes),
        compiler_params=pltpu.CompilerParams(vmem_limit_bytes=24 * 2**20),
    )(*[s.reshape(1) for s in scalars], *arrays, *after)


def split(x):
    high = x.astype(jnp.bfloat16)
    return high, (x - high.astype(jnp.float32)).astype(jnp.bfloat16)


def dot(x, y, dims):
    def one(u, v):
        return lax.dot_general(u, v, (dims, ((), ())), preferred_element_type=jnp.float32)

    return one(x[0], y[0]) + (one(x[0], y[1]) + one(x[1], y[0]))


def block(start_ref, width):
    return pl.ds(pl.multiple_of(start_ref[0], width), width)


def ordered(chip_ref, first_ref, second_ref, body):
    low_first = chip_ref[0] < CHIPS // 2
    pl.when(low_first)(lambda: body(first_ref, second_ref))
    pl.when(jnp.logical_not(low_first))(lambda: body(second_ref, first_ref))


def pair_tile(chip_ref, mine_ref, other_ref, first_ref, second_ref, keep_ref, give_ref):
    def body(lower_ref, upper_ref):
        upper = split(upper_ref[...])
        for start_ref, out_ref in ((other_ref, give_ref), (mine_ref, keep_ref)):
            columns = block(start_ref, out_ref.shape[1])
            out_ref[...] = dot(upper, split(lower_ref[:, columns]), ((0,), (0,)))

    ordered(chip_ref, first_ref, second_ref, body)


def add_tiles(keep_ref, got_ref, out_ref):
    out_ref[...] = (keep_ref[...] + got_ref[...]).reshape(out_ref.shape)


def divide(parts_ref, denominator_ref, out_ref):
    total = (parts_ref[0] + parts_ref[1]) + (parts_ref[2] + parts_ref[3])
    amplitude = total / denominator_ref[...]
    for k in range(CHIPS):
        out_ref[k] = amplitude


def density_parts(chip_ref, mine_ref, other_ref, first_ref, second_ref, amp_ref, swapped_ref, out_1_ref, out_2_ref):
    virt, width = first_ref.shape[1], amp_ref.shape[2]

    def body(lower_ref, upper_ref, for_lower_ref, for_upper_ref):
        upper = split(upper_ref[...])
        total = None
        for start_ref, half_ref in ((mine_ref, amp_ref), (other_ref, swapped_ref)):
            columns = block(start_ref, width)
            amp = split(half_ref[...].reshape(virt, width))
            for_lower_ref[:, columns] = dot(upper, amp, ((1,), (0,)))
            part = dot(split(lower_ref[:, columns]), amp, ((1,), (1,)))
            total = part if total is None else total + part
        for_upper_ref[...] = total

    low_first = chip_ref[0] < CHIPS // 2
    pl.when(low_first)(lambda: body(first_ref, second_ref, out_1_ref, out_2_ref))
    pl.when(jnp.logical_not(low_first))(lambda: body(second_ref, first_ref, out_2_ref, out_1_ref))


def local(factors, occ_energy, virt_energy):
    own = factors[0]
    rows, virt = own.shape
    half, quarter = virt // 2, virt // CHIPS
    occupied = lax.axis_size("occ")
    above, below = meetings(occupied)
    first, second = in_two(above, below)
    groups = [
        [above[level * CHIPS + RING * column + c] for c in range(CHIPS)]
        for column in range(occupied // LEVELS)
        for level in range(LEVELS)
    ]
    mine = lax.axis_index("core") * half
    other = half - mine
    chip = lax.rem(lax.axis_index("z") + CHIPS // 2, CHIPS)

    def shared(x):
        return lax.all_to_all(x, PLACES, 0, 0, axis_index_groups=groups, tiled=True)

    got_1, got_2 = move(own, there(first)), move(own, there(second))
    energies = move(occ_energy, there(first)), move(occ_energy, there(second))
    keep, give = kernel(pair_tile, [(virt, half)] * 2, [chip, mine, other], [got_1, got_2], energies)
    whole = (CHIPS, quarter, half)
    tile = kernel(add_tiles, [whole], [], [keep, core_swap(give)])[0]
    row_energy = lax.dynamic_slice_in_dim(virt_energy, chip * quarter, quarter, 0)
    column_energy = lax.dynamic_slice_in_dim(virt_energy, mine, half, 0)
    denominator = (row_energy - (energies[0] + energies[1]))[:, None] + column_energy[None, :]
    amp = shared(kernel(divide, [whole], [], [shared(tile), denominator])[0])
    part_1, part_2 = kernel(
        density_parts, [(rows, virt)] * 2, [chip, mine, other], [got_1, got_2, amp, core_swap(amp)]
    )
    return (move(part_1, back(first)) + move(part_2, back(second)))[None]


def solution(mesh):
    cube = Mesh(mesh.devices.reshape(mesh.devices.shape[0], CHIPS, 2), (*PLACES, "core"))
    spec = P("occ", ("z", "core"), None)
    return jax.shard_map(local, mesh=cube, in_specs=(spec, P("occ"), P()), out_specs=spec, check_vma=False)
```

```python
import jax
import jax.numpy as jnp
import numpy as np
from jax import lax
from jax.experimental import pallas as pl
from jax.experimental.pallas import tpu as pltpu
from jax.sharding import Mesh, PartitionSpec as P

CHIPS = 4
LEVELS = 3
RING = CHIPS * LEVELS
ROWS = 8
PLACES = ("occ", "z")
SMEM = pl.BlockSpec(memory_space=pltpu.SMEM)
VMEM = pl.BlockSpec(memory_space=pltpu.VMEM)
ANY = pl.BlockSpec(memory_space=pl.ANY)


def meeting(column, level, chunk):
    x, y = divmod(column, ROWS)
    crosses = (chunk + y + level) % 2
    plane = 2 + 2 * (x % 2) + chunk // 2
    return ((x ^ crosses) * ROWS + y) * RING + (level * CHIPS + plane) % RING


def meetings(occupied):
    above, below, groups = [0] * (occupied * CHIPS), [0] * (occupied * CHIPS), []
    for i in range(occupied):
        groups.append([meeting(*divmod(i, LEVELS), chunk) for chunk in range(CHIPS)])
        for chunk, goal in enumerate(groups[-1]):
            above[i * CHIPS + chunk] = goal
            below[(i + 1) % occupied * CHIPS + chunk] = goal
    return above, below, groups


def there(goals):
    return [(place, goal) for place, goal in enumerate(goals)]


def back(goals):
    return [(goal, place) for place, goal in enumerate(goals)]


def move(x, pairs):
    return lax.ppermute(x, PLACES, pairs)


def core_swap(x):
    return lax.ppermute(x, "core", [(0, 1), (1, 0)])


def kernel(body, shapes, scalars, arrays, after=()):
    used = len(scalars) + len(arrays)

    def run(*refs):
        body(*refs[:used], *refs[used + len(after) :])

    return pl.pallas_call(
        run,
        out_shape=[jax.ShapeDtypeStruct(s, jnp.float32) for s in shapes],
        in_specs=[SMEM] * len(scalars) + [VMEM] * len(arrays) + [ANY] * len(after),
        out_specs=[VMEM] * len(shapes),
        compiler_params=pltpu.CompilerParams(vmem_limit_bytes=24 * 2**20),
    )(*[s.reshape(1) for s in scalars], *arrays, *after)


def split(x):
    high = x.astype(jnp.bfloat16)
    return high, (x - high.astype(jnp.float32)).astype(jnp.bfloat16)


def dot(x, y, dims):
    def one(u, v):
        return lax.dot_general(u, v, (dims, ((), ())), preferred_element_type=jnp.float32)

    return one(x[0], y[0]) + (one(x[0], y[1]) + one(x[1], y[0]))


def block(start_ref, width):
    return pl.ds(pl.multiple_of(start_ref[0], width), width)


def pair_tile(mine_ref, other_ref, lower_ref, upper_ref, keep_ref, give_ref):
    width = keep_ref.shape[1]
    upper = split(upper_ref[...])
    for start_ref, out_ref in ((other_ref, give_ref), (mine_ref, keep_ref)):
        out_ref[...] = dot(upper, split(lower_ref[:, block(start_ref, width)]), ((0,), (0,)))


def add_tiles(keep_ref, got_ref, out_ref):
    out_ref[...] = (keep_ref[...] + got_ref[...]).reshape(out_ref.shape)


def divide(parts_ref, denominator_ref, out_ref):
    total = (parts_ref[0] + parts_ref[1]) + (parts_ref[2] + parts_ref[3])
    amplitude = total / denominator_ref[...]
    for k in range(CHIPS):
        out_ref[k] = amplitude


def density_parts(mine_ref, other_ref, lower_ref, upper_ref, amp_ref, swapped_ref, up_ref, down_ref):
    rows, virt = up_ref.shape
    width = amp_ref.shape[2]
    upper = split(upper_ref[...])
    total = None
    for start_ref, half_ref in ((mine_ref, amp_ref), (other_ref, swapped_ref)):
        columns = block(start_ref, width)
        amp = split(half_ref[...].reshape(virt, width))
        down_ref[:, columns] = dot(upper, amp, ((1,), (0,)))
        part = dot(split(lower_ref[:, columns]), amp, ((1,), (1,)))
        total = part if total is None else total + part
    up_ref[...] = total


def local(factors, occ_energy, virt_energy):
    own = factors[0]
    rows, virt = own.shape
    half, quarter = virt // 2, virt // CHIPS
    occupied = lax.axis_size("occ")
    above, below, groups = meetings(occupied)
    order = np.argsort(np.ravel(groups)) % CHIPS
    mine = lax.axis_index("core") * half
    other = half - mine
    place = lax.axis_index("occ") * CHIPS + lax.axis_index("z")
    chip = lax.dynamic_index_in_dim(jnp.asarray(order, jnp.int32), place, keepdims=False)

    def shared(x):
        return lax.all_to_all(x, PLACES, 0, 0, axis_index_groups=groups, tiled=True)

    lower, upper = move(own, there(above)), move(own, there(below))
    energies = move(occ_energy, there(above)), move(occ_energy, there(below))
    keep, give = kernel(pair_tile, [(virt, half)] * 2, [mine, other], [lower, upper], energies)
    whole = (CHIPS, quarter, half)
    tile = kernel(add_tiles, [whole], [], [keep, core_swap(give)])[0]
    row_energy = lax.dynamic_slice_in_dim(virt_energy, chip * quarter, quarter, 0)
    column_energy = lax.dynamic_slice_in_dim(virt_energy, mine, half, 0)
    denominator = (row_energy - (energies[0] + energies[1]))[:, None] + column_energy[None, :]
    amp = shared(kernel(divide, [whole], [], [shared(tile), denominator])[0])
    up, down = kernel(density_parts, [(rows, virt)] * 2, [mine, other], [lower, upper, amp, core_swap(amp)])
    return (move(up, back(below)) + move(down, back(above)))[None]


def solution(mesh):
    cube = Mesh(mesh.devices.reshape(mesh.devices.shape[0], CHIPS, 2), (*PLACES, "core"))
    spec = P("occ", ("z", "core"), None)
    return jax.shard_map(local, mesh=cube, in_specs=(spec, P("occ"), P()), out_specs=spec, check_vma=False)
```

```python
import jax
import jax.numpy as jnp
from jax import lax
from jax.experimental import pallas as pl
from jax.experimental.pallas import tpu as pltpu
from jax.sharding import Mesh, PartitionSpec as P

CHIPS = 4
PLACES = ("occ", "z")
SMEM = pl.BlockSpec(memory_space=pltpu.SMEM)
VMEM = pl.BlockSpec(memory_space=pltpu.VMEM)
ANY = pl.BlockSpec(memory_space=pl.ANY)


def neighbours(occupied):
    goals, groups = [], []
    for i in range(occupied):
        for z in range(CHIPS):
            goals.append((i + (1 if z < CHIPS // 2 else -1)) % occupied * CHIPS + z)
        groups.append([(i if z < CHIPS // 2 else (i - 1) % occupied) * CHIPS + z for z in range(CHIPS)])
    return goals, groups


def move(x, goals):
    return lax.ppermute(x, PLACES, list(enumerate(goals)))


def move_back(x, goals):
    return lax.ppermute(x, PLACES, [(goal, place) for place, goal in enumerate(goals)])


def core_swap(x):
    return lax.ppermute(x, "core", [(0, 1), (1, 0)])


def kernel(body, shapes, scalars, arrays, after=()):
    used = len(scalars) + len(arrays)

    def run(*refs):
        body(*refs[:used], *refs[used + len(after) :])

    return pl.pallas_call(
        run,
        out_shape=[jax.ShapeDtypeStruct(s, jnp.float32) for s in shapes],
        in_specs=[SMEM] * len(scalars) + [VMEM] * len(arrays) + [ANY] * len(after),
        out_specs=[VMEM] * len(shapes),
        compiler_params=pltpu.CompilerParams(vmem_limit_bytes=24 * 2**20),
    )(*[s.reshape(1) for s in scalars], *arrays, *after)


def split(x):
    high = x.astype(jnp.bfloat16)
    return high, (x - high.astype(jnp.float32)).astype(jnp.bfloat16)


def dot(x, y, dims):
    def one(u, v):
        return lax.dot_general(u, v, (dims, ((), ())), preferred_element_type=jnp.float32)

    return one(x[0], y[0]) + (one(x[0], y[1]) + one(x[1], y[0]))


def block(start_ref, width):
    return pl.ds(pl.multiple_of(start_ref[0], width), width)


def by_half(chip_ref, lower_half, upper_half):
    low = chip_ref[0] < CHIPS // 2
    pl.when(low)(lower_half)
    pl.when(jnp.logical_not(low))(upper_half)


def pair_tile(chip_ref, mine_ref, other_ref, own_ref, got_ref, keep_ref, give_ref):
    def body(lower_ref, upper_ref):
        upper = split(upper_ref[...])
        for start_ref, out_ref in ((other_ref, give_ref), (mine_ref, keep_ref)):
            out_ref[...] = dot(upper, split(lower_ref[:, block(start_ref, out_ref.shape[1])]), ((0,), (0,)))

    by_half(chip_ref, lambda: body(got_ref, own_ref), lambda: body(own_ref, got_ref))


def add_tiles(keep_ref, got_ref, out_ref):
    out_ref[...] = (keep_ref[...] + got_ref[...]).reshape(out_ref.shape)


def divide(parts_ref, denominator_ref, out_ref):
    total = (parts_ref[0] + parts_ref[1]) + (parts_ref[2] + parts_ref[3])
    amplitude = total / denominator_ref[...]
    for k in range(CHIPS):
        out_ref[k] = amplitude


def times_upper(mine_ref, other_ref, lower_ref, amp_ref, swapped_ref, out_ref):
    virt, width = lower_ref.shape[1], amp_ref.shape[2]
    total = None
    for start_ref, half_ref in ((mine_ref, amp_ref), (other_ref, swapped_ref)):
        amp = split(half_ref[...].reshape(virt, width))
        part = dot(split(lower_ref[:, block(start_ref, width)]), amp, ((1,), (1,)))
        total = part if total is None else total + part
    out_ref[...] = total


def times_lower(mine_ref, other_ref, upper_ref, amp_ref, swapped_ref, out_ref):
    virt, width = upper_ref.shape[1], amp_ref.shape[2]
    upper = split(upper_ref[...])
    for start_ref, half_ref in ((mine_ref, amp_ref), (other_ref, swapped_ref)):
        amp = split(half_ref[...].reshape(virt, width))
        out_ref[:, block(start_ref, width)] = dot(upper, amp, ((1,), (0,)))


def part_away(chip_ref, mine_ref, other_ref, own_ref, amp_ref, swapped_ref, out_ref):
    rest = (mine_ref, other_ref, own_ref, amp_ref, swapped_ref, out_ref)
    by_half(chip_ref, lambda: times_lower(*rest), lambda: times_upper(*rest))


def part_here(chip_ref, mine_ref, other_ref, got_ref, amp_ref, swapped_ref, out_ref):
    rest = (mine_ref, other_ref, got_ref, amp_ref, swapped_ref, out_ref)
    by_half(chip_ref, lambda: times_upper(*rest), lambda: times_lower(*rest))


def local(factors, occ_energy, virt_energy):
    own = factors[0]
    rows, virt = own.shape
    half, quarter = virt // 2, virt // CHIPS
    goals, groups = neighbours(lax.axis_size("occ"))
    mine = lax.axis_index("core") * half
    other = half - mine
    chip = lax.axis_index("z")
    at = [chip, mine, other]

    def shared(x):
        return lax.all_to_all(x, PLACES, 0, 0, axis_index_groups=groups, tiled=True)

    got = move(own, goals)
    got_energy = move(jnp.broadcast_to(occ_energy, (8, 128)), goals)
    keep, give = kernel(pair_tile, [(virt, half)] * 2, at, [own, got], [got_energy])
    whole = (CHIPS, quarter, half)
    tile = kernel(add_tiles, [whole], [], [keep, core_swap(give)])[0]
    row_energy = lax.dynamic_slice_in_dim(virt_energy, chip * quarter, quarter, 0)
    column_energy = lax.dynamic_slice_in_dim(virt_energy, mine, half, 0)
    denominator = (row_energy - (occ_energy + got_energy[0, 0]))[:, None] + column_energy[None, :]
    amp = shared(kernel(divide, [whole], [], [shared(tile), denominator])[0])
    swapped = core_swap(amp)
    away = kernel(part_away, [(rows, virt)], at, [own, amp, swapped])[0]
    here = kernel(part_here, [(rows, virt)], at, [got, amp, swapped], [away])[0]
    return (here + move_back(away, goals))[None]


def solution(mesh):
    cube = Mesh(mesh.devices.reshape(mesh.devices.shape[0], CHIPS, 2), (*PLACES, "core"))
    spec = P("occ", ("z", "core"), None)
    return jax.shard_map(local, mesh=cube, in_specs=(spec, P("occ"), P()), out_specs=spec, check_vma=False)
```

```python
import jax
import jax.numpy as jnp
from jax import lax
from jax.experimental import pallas as pl
from jax.experimental.pallas import tpu as pltpu
from jax.sharding import Mesh, PartitionSpec as P

CHIPS = 4
LEVELS = 3
RING = CHIPS * LEVELS
PLACES = ("occ", "z")
SMEM = pl.BlockSpec(memory_space=pltpu.SMEM)
VMEM = pl.BlockSpec(memory_space=pltpu.VMEM)
ANY = pl.BlockSpec(memory_space=pl.ANY)


def meetings(occupied):
    above, below, groups = [0] * (occupied * CHIPS), [0] * (occupied * CHIPS), []
    for i in range(occupied):
        column, level = divmod(i, LEVELS)
        groups.append([column * RING + (level * CHIPS + c + CHIPS // 2) % RING for c in range(CHIPS)])
        for c, goal in enumerate(groups[-1]):
            above[i * CHIPS + c] = goal
            below[(i + 1) % occupied * CHIPS + c] = goal
    return above, below, groups


def there(goals):
    return [(place, goal) for place, goal in enumerate(goals)]


def back(goals):
    return [(goal, place) for place, goal in enumerate(goals)]


def move(x, pairs):
    return lax.ppermute(x, PLACES, pairs)


def core_swap(x):
    return lax.ppermute(x, "core", [(0, 1), (1, 0)])


def kernel(body, shapes, scalars, arrays, after=()):
    used = len(scalars) + len(arrays)

    def run(*refs):
        body(*refs[:used], *refs[used + len(after) :])

    return pl.pallas_call(
        run,
        out_shape=[jax.ShapeDtypeStruct(s, jnp.float32) for s in shapes],
        in_specs=[SMEM] * len(scalars) + [VMEM] * len(arrays) + [ANY] * len(after),
        out_specs=[VMEM] * len(shapes),
        compiler_params=pltpu.CompilerParams(vmem_limit_bytes=24 * 2**20),
    )(*[s.reshape(1) for s in scalars], *arrays, *after)


def split(x):
    high = x.astype(jnp.bfloat16)
    return high, (x - high.astype(jnp.float32)).astype(jnp.bfloat16)


def dot(x, y, dims):
    def one(u, v):
        return lax.dot_general(u, v, (dims, ((), ())), preferred_element_type=jnp.float32)

    return one(x[0], y[0]) + (one(x[0], y[1]) + one(x[1], y[0]))


def block(start_ref, width):
    return pl.ds(pl.multiple_of(start_ref[0], width), width)


def pair_tile(start_ref, lower_ref, upper_ref, out_ref):
    lower = split(lower_ref[:, block(start_ref, out_ref.shape[1])])
    out_ref[...] = dot(split(upper_ref[...]), lower, ((0,), (0,)))


def add_tiles(keep_ref, got_ref, out_ref):
    out_ref[...] = (keep_ref[...] + got_ref[...]).reshape(out_ref.shape)


def divide(parts_ref, denominator_ref, out_ref):
    total = (parts_ref[0] + parts_ref[1]) + (parts_ref[2] + parts_ref[3])
    amplitude = total / denominator_ref[...]
    for k in range(CHIPS):
        out_ref[k] = amplitude


def density_parts(mine_ref, other_ref, lower_ref, upper_ref, amp_ref, swapped_ref, up_ref, down_ref):
    rows, virt = up_ref.shape
    width = amp_ref.shape[2]
    upper = split(upper_ref[...])
    total = None
    for start_ref, half_ref in ((mine_ref, amp_ref), (other_ref, swapped_ref)):
        columns = block(start_ref, width)
        amp = split(half_ref[...].reshape(virt, width))
        down_ref[:, columns] = dot(upper, amp, ((1,), (0,)))
        part = dot(split(lower_ref[:, columns]), amp, ((1,), (1,)))
        total = part if total is None else total + part
    up_ref[...] = total


def local(factors, occ_energy, virt_energy):
    own = factors[0]
    rows, virt = own.shape
    half, quarter = virt // 2, virt // CHIPS
    occupied = lax.axis_size("occ")
    above, below, groups = meetings(occupied)
    mine = lax.axis_index("core") * half
    other = half - mine
    chip = lax.rem(lax.axis_index("z") + CHIPS // 2, CHIPS)

    def shared(x):
        return lax.all_to_all(x, PLACES, 0, 0, axis_index_groups=groups, tiled=True)

    lower, upper = move(own, there(above)), move(own, there(below))
    energy = jnp.broadcast_to(occ_energy, (8, 128))
    energies = move(energy, there(above)), move(energy, there(below))
    give = kernel(pair_tile, [(virt, half)], [other], [lower, upper], energies)[0]
    keep = kernel(pair_tile, [(virt, half)], [mine], [lower, upper], [give])[0]
    whole = (CHIPS, quarter, half)
    tile = kernel(add_tiles, [whole], [], [keep, core_swap(give)])[0]
    row_energy = lax.dynamic_slice_in_dim(virt_energy, chip * quarter, quarter, 0)
    column_energy = lax.dynamic_slice_in_dim(virt_energy, mine, half, 0)
    denominator = (row_energy - (energies[0][0, 0] + energies[1][0, 0]))[:, None] + column_energy[None, :]
    amp = shared(kernel(divide, [whole], [], [shared(tile), denominator])[0])
    swapped = core_swap(amp)
    up, down = kernel(density_parts, [(rows, virt)] * 2, [mine, other], [lower, upper, amp, swapped])
    return (move(up, back(below)) + move(down, back(above)))[None]


def solution(mesh):
    cube = Mesh(mesh.devices.reshape(mesh.devices.shape[0], CHIPS, 2), (*PLACES, "core"))
    spec = P("occ", ("z", "core"), None)
    return jax.shard_map(local, mesh=cube, in_specs=(spec, P("occ"), P()), out_specs=spec, check_vma=False)
```

```python
import jax
import jax.numpy as jnp
from jax import lax
from jax.experimental import pallas as pl
from jax.experimental.pallas import tpu as pltpu
from jax.sharding import Mesh, PartitionSpec as P

CHIPS = 4
LEVELS = 3
RING = CHIPS * LEVELS
PLACES = ("occ", "z")
SMEM = pl.BlockSpec(memory_space=pltpu.SMEM)
VMEM = pl.BlockSpec(memory_space=pltpu.VMEM)
ANY = pl.BlockSpec(memory_space=pl.ANY)


def meetings(occupied):
    above, below, groups = [0] * (occupied * CHIPS), [0] * (occupied * CHIPS), []
    for i in range(occupied):
        column, level = divmod(i, LEVELS)
        groups.append([column * RING + (level * CHIPS + c + CHIPS // 2) % RING for c in range(CHIPS)])
        for c, goal in enumerate(groups[-1]):
            above[i * CHIPS + c] = goal
            below[(i + 1) % occupied * CHIPS + c] = goal
    return above, below, groups


def there(goals):
    return [(place, goal) for place, goal in enumerate(goals)]


def back(goals):
    return [(goal, place) for place, goal in enumerate(goals)]


def move(x, pairs):
    return lax.ppermute(x, PLACES, pairs)


def core_swap(x):
    return lax.ppermute(x, "core", [(0, 1), (1, 0)])


def kernel(body, shapes, scalars, arrays, after=()):
    used = len(scalars) + len(arrays)

    def run(*refs):
        body(*refs[:used], *refs[used + len(after) :])

    return pl.pallas_call(
        run,
        out_shape=[jax.ShapeDtypeStruct(s, jnp.float32) for s in shapes],
        in_specs=[SMEM] * len(scalars) + [VMEM] * len(arrays) + [ANY] * len(after),
        out_specs=[VMEM] * len(shapes),
        compiler_params=pltpu.CompilerParams(vmem_limit_bytes=24 * 2**20),
    )(*[s.reshape(1) for s in scalars], *arrays, *after)


def split(x):
    high = x.astype(jnp.bfloat16)
    return high, (x - high.astype(jnp.float32)).astype(jnp.bfloat16)


def dot(x, y, dims):
    def one(u, v):
        return lax.dot_general(u, v, (dims, ((), ())), preferred_element_type=jnp.float32)

    return one(x[0], y[0]) + (one(x[0], y[1]) + one(x[1], y[0]))


def block(start_ref, width):
    return pl.ds(pl.multiple_of(start_ref[0], width), width)


def pair_tile(start_ref, lower_ref, upper_ref, out_ref):
    lower = split(lower_ref[:, block(start_ref, out_ref.shape[1])])
    out_ref[...] = dot(split(upper_ref[...]), lower, ((0,), (0,)))


def add_tiles(keep_ref, got_ref, out_ref):
    out_ref[...] = (keep_ref[...] + got_ref[...]).reshape(out_ref.shape)


def divide(parts_ref, sums_ref, energy_ref, other_energy_ref, out_ref):
    total = (parts_ref[0] + parts_ref[1]) + (parts_ref[2] + parts_ref[3])
    amplitude = total / (sums_ref[...] - (energy_ref[:1, :1] + other_energy_ref[:1, :1]))
    for k in range(CHIPS):
        out_ref[k] = amplitude


def density_parts(mine_ref, other_ref, lower_ref, upper_ref, amp_ref, swapped_ref, up_ref, down_ref):
    rows, virt = up_ref.shape
    width = amp_ref.shape[2]
    upper = split(upper_ref[...])
    total = None
    for start_ref, half_ref in ((mine_ref, amp_ref), (other_ref, swapped_ref)):
        columns = block(start_ref, width)
        amp = split(half_ref[...].reshape(virt, width))
        down_ref[:, columns] = dot(upper, amp, ((1,), (0,)))
        part = dot(split(lower_ref[:, columns]), amp, ((1,), (1,)))
        total = part if total is None else total + part
    up_ref[...] = total


def local(factors, occ_energy, virt_energy):
    own = factors[0]
    rows, virt = own.shape
    half, quarter = virt // 2, virt // CHIPS
    occupied = lax.axis_size("occ")
    above, below, groups = meetings(occupied)
    mine = lax.axis_index("core") * half
    other = half - mine
    chip = lax.rem(lax.axis_index("z") + CHIPS // 2, CHIPS)

    def shared(x):
        return lax.all_to_all(x, PLACES, 0, 0, axis_index_groups=groups, tiled=True)

    lower, upper = move(own, there(above)), move(own, there(below))
    energy = jnp.broadcast_to(occ_energy, (8, 128))
    energies = move(energy, there(above)), move(energy, there(below))
    row_energy = lax.dynamic_slice_in_dim(virt_energy, chip * quarter, quarter, 0)
    column_energy = lax.dynamic_slice_in_dim(virt_energy, mine, half, 0)
    sums = row_energy[:, None] + column_energy[None, :]
    give = kernel(pair_tile, [(virt, half)], [other], [lower, upper], [*energies, sums])[0]
    keep = kernel(pair_tile, [(virt, half)], [mine], [lower, upper], [give])[0]
    whole = (CHIPS, quarter, half)
    tile = kernel(add_tiles, [whole], [], [keep, core_swap(give)])[0]
    amp = shared(kernel(divide, [whole], [], [shared(tile), sums, *energies])[0])
    swapped = core_swap(amp)
    up, down = kernel(density_parts, [(rows, virt)] * 2, [mine, other], [lower, upper, amp, swapped])
    return (move(up, back(below)) + move(down, back(above)))[None]


def solution(mesh):
    cube = Mesh(mesh.devices.reshape(mesh.devices.shape[0], CHIPS, 2), (*PLACES, "core"))
    spec = P("occ", ("z", "core"), None)
    return jax.shard_map(local, mesh=cube, in_specs=(spec, P("occ"), P()), out_specs=spec, check_vma=False)
```

```python
import jax
import jax.numpy as jnp
from jax import lax
from jax.experimental import pallas as pl
from jax.experimental.pallas import tpu as pltpu
from jax.sharding import Mesh, PartitionSpec as P

CHIPS = 4
LEVELS = 3
RING = CHIPS * LEVELS
PLACES = ("occ", "z")
PLANES = (3, 5, 2, 4)
SMEM = pl.BlockSpec(memory_space=pltpu.SMEM)
VMEM = pl.BlockSpec(memory_space=pltpu.VMEM)
ANY = pl.BlockSpec(memory_space=pl.ANY)


def meetings(occupied):
    above, below, groups = [0] * (occupied * CHIPS), [0] * (occupied * CHIPS), []
    for i in range(occupied):
        column, level = divmod(i, LEVELS)
        groups.append([column * RING + (level * CHIPS + plane) % RING for plane in PLANES])
        for c, goal in enumerate(groups[-1]):
            above[i * CHIPS + c] = goal
            below[(i + 1) % occupied * CHIPS + c] = goal
    return above, below, groups


def there(goals):
    return [(place, goal) for place, goal in enumerate(goals)]


def back(goals):
    return [(goal, place) for place, goal in enumerate(goals)]


def move(x, pairs):
    return lax.ppermute(x, PLACES, pairs)


def core_swap(x):
    return lax.ppermute(x, "core", [(0, 1), (1, 0)])


def kernel(body, shapes, scalars, arrays, after=()):
    used = len(scalars) + len(arrays)

    def run(*refs):
        body(*refs[:used], *refs[used + len(after) :])

    return pl.pallas_call(
        run,
        out_shape=[jax.ShapeDtypeStruct(s, jnp.float32) for s in shapes],
        in_specs=[SMEM] * len(scalars) + [VMEM] * len(arrays) + [ANY] * len(after),
        out_specs=[VMEM] * len(shapes),
        compiler_params=pltpu.CompilerParams(vmem_limit_bytes=24 * 2**20),
    )(*[s.reshape(1) for s in scalars], *arrays, *after)


def split(x):
    high = x.astype(jnp.bfloat16)
    return high, (x - high.astype(jnp.float32)).astype(jnp.bfloat16)


def dot(x, y, dims):
    def one(u, v):
        return lax.dot_general(u, v, (dims, ((), ())), preferred_element_type=jnp.float32)

    return one(x[0], y[0]) + (one(x[0], y[1]) + one(x[1], y[0]))


def block(start_ref, width):
    return pl.ds(pl.multiple_of(start_ref[0], width), width)


def pair_tile(start_ref, lower_ref, upper_ref, out_ref):
    lower = split(lower_ref[:, block(start_ref, out_ref.shape[1])])
    out_ref[...] = dot(split(upper_ref[...]), lower, ((0,), (0,)))


def add_tiles(keep_ref, got_ref, out_ref):
    out_ref[...] = (keep_ref[...] + got_ref[...]).reshape(out_ref.shape)


def divide(parts_ref, sums_ref, energy_ref, other_energy_ref, out_ref):
    total = (parts_ref[0] + parts_ref[1]) + (parts_ref[2] + parts_ref[3])
    amplitude = total / (sums_ref[...] - (energy_ref[:1, :1] + other_energy_ref[:1, :1]))
    for k in range(CHIPS):
        out_ref[k] = amplitude


def density_parts(mine_ref, other_ref, lower_ref, upper_ref, amp_ref, swapped_ref, up_ref, down_ref):
    rows, virt = up_ref.shape
    width = amp_ref.shape[2]
    upper = split(upper_ref[...])
    total = None
    for start_ref, half_ref in ((mine_ref, amp_ref), (other_ref, swapped_ref)):
        columns = block(start_ref, width)
        amp = split(half_ref[...].reshape(virt, width))
        down_ref[:, columns] = dot(upper, amp, ((1,), (0,)))
        part = dot(split(lower_ref[:, columns]), amp, ((1,), (1,)))
        total = part if total is None else total + part
    up_ref[...] = total


def local(factors, occ_energy, virt_energy):
    own = factors[0]
    rows, virt = own.shape
    half, quarter = virt // 2, virt // CHIPS
    occupied = lax.axis_size("occ")
    above, below, groups = meetings(occupied)
    mine = lax.axis_index("core") * half
    other = half - mine
    chip = lax.dynamic_index_in_dim(jnp.asarray((3, 1, 2, 0), jnp.int32), lax.axis_index("z"), keepdims=False)

    def shared(x):
        return lax.all_to_all(x, PLACES, 0, 0, axis_index_groups=groups, tiled=True)

    lower, upper = move(own, there(above)), move(own, there(below))
    energy = jnp.broadcast_to(occ_energy, (8, 128))
    energies = move(energy, there(above)), move(energy, there(below))
    row_energy = lax.dynamic_slice_in_dim(virt_energy, chip * quarter, quarter, 0)
    column_energy = lax.dynamic_slice_in_dim(virt_energy, mine, half, 0)
    sums = row_energy[:, None] + column_energy[None, :]
    give = kernel(pair_tile, [(virt, half)], [other], [lower, upper], [*energies, sums])[0]
    keep = kernel(pair_tile, [(virt, half)], [mine], [lower, upper], [give])[0]
    whole = (CHIPS, quarter, half)
    tile = kernel(add_tiles, [whole], [], [keep, core_swap(give)])[0]
    amp = shared(kernel(divide, [whole], [], [shared(tile), sums, *energies])[0])
    swapped = core_swap(amp)
    up, down = kernel(density_parts, [(rows, virt)] * 2, [mine, other], [lower, upper, amp, swapped])
    return (move(up, back(below)) + move(down, back(above)))[None]


def solution(mesh):
    cube = Mesh(mesh.devices.reshape(mesh.devices.shape[0], CHIPS, 2), (*PLACES, "core"))
    spec = P("occ", ("z", "core"), None)
    return jax.shard_map(local, mesh=cube, in_specs=(spec, P("occ"), P()), out_specs=spec, check_vma=False)
```

```python
import jax
import jax.numpy as jnp
from jax import lax
from jax.experimental import pallas as pl
from jax.experimental.pallas import tpu as pltpu
from jax.sharding import Mesh, PartitionSpec as P

CHIPS = 4
LEVELS = 3
RING = CHIPS * LEVELS
PLACES = ("occ", "z")
PLANES = (3, 5, 2, 4)
SMEM = pl.BlockSpec(memory_space=pltpu.SMEM)
VMEM = pl.BlockSpec(memory_space=pltpu.VMEM)
ANY = pl.BlockSpec(memory_space=pl.ANY)


def meetings(occupied):
    above, below, groups = [0] * (occupied * CHIPS), [0] * (occupied * CHIPS), []
    for i in range(occupied):
        column, level = divmod(i, LEVELS)
        groups.append([column * RING + (level * CHIPS + plane) % RING for plane in PLANES])
        for c, goal in enumerate(groups[-1]):
            above[i * CHIPS + c] = goal
            below[(i + 1) % occupied * CHIPS + c] = goal
    return above, below, groups


def there(goals):
    return [(place, goal) for place, goal in enumerate(goals)]


def back(goals):
    return [(goal, place) for place, goal in enumerate(goals)]


def move(x, pairs):
    return lax.ppermute(x, PLACES, pairs)


def core_swap(x):
    return lax.ppermute(x, "core", [(0, 1), (1, 0)])


def kernel(body, shapes, scalars, arrays, after=()):
    used = len(scalars) + len(arrays)

    def run(*refs):
        body(*refs[:used], *refs[used + len(after) :])

    return pl.pallas_call(
        run,
        out_shape=[jax.ShapeDtypeStruct(s, jnp.float32) for s in shapes],
        in_specs=[SMEM] * len(scalars) + [VMEM] * len(arrays) + [ANY] * len(after),
        out_specs=[VMEM] * len(shapes),
        compiler_params=pltpu.CompilerParams(vmem_limit_bytes=24 * 2**20),
    )(*[s.reshape(1) for s in scalars], *arrays, *after)


def split(x):
    high = x.astype(jnp.bfloat16)
    return high, (x - high.astype(jnp.float32)).astype(jnp.bfloat16)


def dot(x, y, dims):
    def one(u, v):
        return lax.dot_general(u, v, (dims, ((), ())), preferred_element_type=jnp.float32)

    return one(x[0], y[0]) + (one(x[0], y[1]) + one(x[1], y[0]))


def block(start_ref, width):
    return pl.ds(pl.multiple_of(start_ref[0], width), width)


def pair_tile(start_ref, lower_ref, upper_ref, out_ref):
    lower = split(lower_ref[:, block(start_ref, out_ref.shape[1])])
    out_ref[...] = dot(split(upper_ref[...]), lower, ((0,), (0,)))


def add_tiles(keep_ref, got_ref, out_ref):
    out_ref[...] = (keep_ref[...] + got_ref[...]).reshape(out_ref.shape)


def divide(parts_ref, sums_ref, energy_ref, other_energy_ref, out_ref):
    total = (parts_ref[0] + parts_ref[1]) + (parts_ref[2] + parts_ref[3])
    amplitude = total / (sums_ref[...] - (energy_ref[:1, :1] + other_energy_ref[:1, :1]))
    for k in range(CHIPS):
        out_ref[k] = amplitude


def half_density(start_ref, lower_ref, upper_ref, half_ref):
    amp = split(half_ref[...].reshape(lower_ref.shape[1], half_ref.shape[2]))
    columns = block(start_ref, half_ref.shape[2])
    return dot(split(lower_ref[:, columns]), amp, ((1,), (1,))), dot(split(upper_ref[...]), amp, ((1,), (0,)))


def first_half(mine_ref, lower_ref, upper_ref, amp_ref, up_ref, down_ref):
    up_ref[...], down_ref[...] = half_density(mine_ref, lower_ref, upper_ref, amp_ref)


def density_parts(mine_ref, other_ref, lower_ref, upper_ref, swapped_ref, half_up_ref, half_down_ref, up_ref, down_ref):
    width = swapped_ref.shape[2]
    up, down = half_density(other_ref, lower_ref, upper_ref, swapped_ref)
    up_ref[...] = half_up_ref[...] + up
    down_ref[:, block(mine_ref, width)] = half_down_ref[...]
    down_ref[:, block(other_ref, width)] = down


def local(factors, occ_energy, virt_energy):
    own = factors[0]
    rows, virt = own.shape
    half, quarter = virt // 2, virt // CHIPS
    occupied = lax.axis_size("occ")
    above, below, groups = meetings(occupied)
    mine = lax.axis_index("core") * half
    other = half - mine
    chip = lax.dynamic_index_in_dim(jnp.asarray((3, 1, 2, 0), jnp.int32), lax.axis_index("z"), keepdims=False)

    def shared(x):
        return lax.all_to_all(x, PLACES, 0, 0, axis_index_groups=groups, tiled=True)

    lower, upper = move(own, there(above)), move(own, there(below))
    energy = jnp.broadcast_to(occ_energy, (8, 128))
    energies = move(energy, there(above)), move(energy, there(below))
    row_energy = lax.dynamic_slice_in_dim(virt_energy, chip * quarter, quarter, 0)
    column_energy = lax.dynamic_slice_in_dim(virt_energy, mine, half, 0)
    sums = row_energy[:, None] + column_energy[None, :]
    give = kernel(pair_tile, [(virt, half)], [other], [lower, upper], [*energies, sums])[0]
    keep = kernel(pair_tile, [(virt, half)], [mine], [lower, upper], [give])[0]
    whole = (CHIPS, quarter, half)
    tile = kernel(add_tiles, [whole], [], [keep, core_swap(give)])[0]
    amp = shared(kernel(divide, [whole], [], [shared(tile), sums, *energies])[0])
    swapped = core_swap(amp)
    halves = kernel(first_half, [(rows, virt), (rows, half)], [mine], [lower, upper, amp])
    up, down = kernel(density_parts, [(rows, virt)] * 2, [mine, other], [lower, upper, swapped, *halves])
    return (move(up, back(below)) + move(down, back(above)))[None]


def solution(mesh):
    cube = Mesh(mesh.devices.reshape(mesh.devices.shape[0], CHIPS, 2), (*PLACES, "core"))
    spec = P("occ", ("z", "core"), None)
    return jax.shard_map(local, mesh=cube, in_specs=(spec, P("occ"), P()), out_specs=spec, check_vma=False)
```

```python
import jax
import jax.numpy as jnp
from jax import lax
from jax.experimental import pallas as pl
from jax.experimental.pallas import tpu as pltpu
from jax.sharding import Mesh, PartitionSpec as P

CHIPS = 4
LEVELS = 3
RING = CHIPS * LEVELS
PLACES = ("occ", "z")
PLANES = (3, 5, 2, 4)
SMEM = pl.BlockSpec(memory_space=pltpu.SMEM)
VMEM = pl.BlockSpec(memory_space=pltpu.VMEM)
ANY = pl.BlockSpec(memory_space=pl.ANY)


def meetings(occupied):
    above, below, groups = [0] * (occupied * CHIPS), [0] * (occupied * CHIPS), []
    for i in range(occupied):
        column, level = divmod(i, LEVELS)
        groups.append([column * RING + (level * CHIPS + plane) % RING for plane in PLANES])
        for c, goal in enumerate(groups[-1]):
            above[i * CHIPS + c] = goal
            below[(i + 1) % occupied * CHIPS + c] = goal
    return above, below, groups


def there(goals):
    return [(place, goal) for place, goal in enumerate(goals)]


def back(goals):
    return [(goal, place) for place, goal in enumerate(goals)]


def move(x, pairs):
    return lax.ppermute(x, PLACES, pairs)


def core_swap(x):
    return lax.ppermute(x, "core", [(0, 1), (1, 0)])


def kernel(body, shapes, scalars, arrays, after=(), dtype=jnp.float32):
    used = len(scalars) + len(arrays)

    def run(*refs):
        body(*refs[:used], *refs[used + len(after) :])

    return pl.pallas_call(
        run,
        out_shape=[jax.ShapeDtypeStruct(s, dtype) for s in shapes],
        in_specs=[SMEM] * len(scalars) + [VMEM] * len(arrays) + [ANY] * len(after),
        out_specs=[VMEM] * len(shapes),
        compiler_params=pltpu.CompilerParams(vmem_limit_bytes=24 * 2**20),
    )(*[s.reshape(1) for s in scalars], *arrays, *after)


def split(x):
    high = x.astype(jnp.bfloat16)
    return high, (x - high.astype(jnp.float32)).astype(jnp.bfloat16)


def dot(x, y, dims):
    def one(u, v):
        return lax.dot_general(u, v, (dims, ((), ())), preferred_element_type=jnp.float32)

    return one(x[0], y[0]) + (one(x[0], y[1]) + one(x[1], y[0]))


def block(start_ref, width):
    return pl.ds(pl.multiple_of(start_ref[0], width), width)


def pair_tile(start_ref, lower_ref, upper_ref, out_ref):
    lower = split(lower_ref[:, block(start_ref, out_ref.shape[1])])
    out_ref[...] = dot(split(upper_ref[...]), lower, ((0,), (0,)))


def split_slabs(lower_ref, upper_ref, *out_refs):
    out_refs[0][...], out_refs[1][...] = split(lower_ref[...])
    out_refs[2][...], out_refs[3][...] = split(upper_ref[...])


def kept_tile(start_ref, lower_high_ref, lower_low_ref, upper_high_ref, upper_low_ref, out_ref):
    columns = block(start_ref, out_ref.shape[1])
    lower = lower_high_ref[:, columns], lower_low_ref[:, columns]
    out_ref[...] = dot((upper_high_ref[...], upper_low_ref[...]), lower, ((0,), (0,)))


def add_tiles(keep_ref, got_ref, out_ref):
    out_ref[...] = (keep_ref[...] + got_ref[...]).reshape(out_ref.shape)


def divide(parts_ref, sums_ref, energy_ref, other_energy_ref, out_ref):
    total = (parts_ref[0] + parts_ref[1]) + (parts_ref[2] + parts_ref[3])
    amplitude = total / (sums_ref[...] - (energy_ref[:1, :1] + other_energy_ref[:1, :1]))
    for k in range(CHIPS):
        out_ref[k] = amplitude


def half_density(start_ref, lower_refs, upper_refs, half_ref):
    amp = split(half_ref[...].reshape(lower_refs[0].shape[1], half_ref.shape[2]))
    columns = block(start_ref, half_ref.shape[2])
    lower, upper = [ref[:, columns] for ref in lower_refs], [ref[...] for ref in upper_refs]
    return dot(lower, amp, ((1,), (1,))), dot(upper, amp, ((1,), (0,)))


def first_half(mine_ref, lower_high, lower_low, upper_high, upper_low, amp_ref, up_ref, down_ref):
    up_ref[...], down_ref[...] = half_density(mine_ref, (lower_high, lower_low), (upper_high, upper_low), amp_ref)


def density_parts(mine_ref, other_ref, lower_high, lower_low, upper_high, upper_low, swapped_ref, *refs):
    half_up_ref, half_down_ref, up_ref, down_ref = refs
    width = swapped_ref.shape[2]
    up, down = half_density(other_ref, (lower_high, lower_low), (upper_high, upper_low), swapped_ref)
    up_ref[...] = half_up_ref[...] + up
    down_ref[:, block(mine_ref, width)] = half_down_ref[...]
    down_ref[:, block(other_ref, width)] = down


def local(factors, occ_energy, virt_energy):
    own = factors[0]
    rows, virt = own.shape
    half, quarter = virt // 2, virt // CHIPS
    occupied = lax.axis_size("occ")
    above, below, groups = meetings(occupied)
    mine = lax.axis_index("core") * half
    other = half - mine
    chip = lax.dynamic_index_in_dim(jnp.asarray((3, 1, 2, 0), jnp.int32), lax.axis_index("z"), keepdims=False)

    def shared(x):
        return lax.all_to_all(x, PLACES, 0, 0, axis_index_groups=groups, tiled=True)

    lower, upper = move(own, there(above)), move(own, there(below))
    energy = jnp.broadcast_to(occ_energy, (8, 128))
    energies = move(energy, there(above)), move(energy, there(below))
    row_energy = lax.dynamic_slice_in_dim(virt_energy, chip * quarter, quarter, 0)
    column_energy = lax.dynamic_slice_in_dim(virt_energy, mine, half, 0)
    sums = row_energy[:, None] + column_energy[None, :]
    give = kernel(pair_tile, [(virt, half)], [other], [lower, upper], [*energies, sums])[0]
    slabs = kernel(split_slabs, [(rows, virt)] * 4, [], [lower, upper], [give], jnp.bfloat16)
    keep = kernel(kept_tile, [(virt, half)], [mine], slabs)[0]
    whole = (CHIPS, quarter, half)
    tile = kernel(add_tiles, [whole], [], [keep, core_swap(give)])[0]
    amp = shared(kernel(divide, [whole], [], [shared(tile), sums, *energies])[0])
    swapped = core_swap(amp)
    halves = kernel(first_half, [(rows, virt), (rows, half)], [mine], [*slabs, amp])
    up, down = kernel(density_parts, [(rows, virt)] * 2, [mine, other], [*slabs, swapped, *halves])
    return (move(up, back(below)) + move(down, back(above)))[None]


def solution(mesh):
    cube = Mesh(mesh.devices.reshape(mesh.devices.shape[0], CHIPS, 2), (*PLACES, "core"))
    spec = P("occ", ("z", "core"), None)
    return jax.shard_map(local, mesh=cube, in_specs=(spec, P("occ"), P()), out_specs=spec, check_vma=False)
```
